256 devices in a mesh: step: 32 (over y, x, z_hi), seq: 8 (over z_lo, core).
Axes of the slice: x: 4, y: 4, z: 8 (z_hi: 2, z_lo: 4; z = z_hi * 4 + z_lo), core: 2. Of those that a mesh axis runs over, the one named last changes fastest.
Arguments:
- trajectory: float32 [32, 4, 256, 3072], P('step', None, 'seq'), may hold values from -6 to 6
- timesteps: int32 [33], replicated, may hold values from 0 to 65, as said below
- offset: int32 [4], replicated, may hold values from 0 to 31, as said below
- mod_table: float32 [66, 3, 3072], replicated, may hold values from -4 to 4
- w_qkv: bfloat16 [3072, 6144], P('step', 'seq'), may hold values from -0.109375 to 0.109375
- w_out: bfloat16 [2048, 3072], P('seq', 'step'), may hold values from -0.25 to 0.25
- query_gain: float32 [128], replicated, may hold values from 1 to 3
- k_gain: float32 [128], replicated, may hold values from 1 to 3
Outputs:
- next_states: float32 [32, 4, 256, 3072], P('step', None, 'seq')
The draws below stay inside these ranges and needn't reach their ends.
Inputs may be any that keep to these rules, and one draw needn't show every extreme that they name: `timesteps`: strictly rising; first entry 0, last entry 65. Some sequence has offset 0 and another has offset 32 - 1.
All inputs are finite; a program needn't handle non-finite values.
Results may differ from the reference program's by a relative error of at most 0.0065.
Values may be sent and summed in bfloat16 or wider, within the bound.
No kernel may reach another device: no remote copies, remote signals or barrier semaphores. Data moves between devices by JAX's collectives and lax.ppermute only.
A program may use at most 128 MiB of HBM per device.

```python
import math
import jax
import jax.numpy as jnp
from jax import lax

D = 3072
HEADS = 16
HEAD_DIM = 128
SEQS = 4
SEQUENCE_TOKENS = 256
STEPS = 32
TOTAL = 66


def draw_timesteps(key, part):
    key = jax.random.fold_in(key, 7)
    shuffled = jax.random.permutation(key, 2 * STEPS).astype(jnp.int32) + 1
    inner = jnp.sort(shuffled[:STEPS - 1]).astype(jnp.int32)
    first = jnp.zeros((1,), jnp.int32)
    last = jnp.full((1,), 2 * STEPS + 1, jnp.int32)
    return jnp.concatenate([first, inner, last]).astype(jnp.int32)


def draw_offset(key, part):
    key = jax.random.fold_in(key, 11)
    order_key, value_key = jax.random.split(key)
    order = jax.random.permutation(order_key, SEQS).astype(jnp.int32)
    chosen = jax.random.randint(value_key, (SEQS,), 0, STEPS).astype(jnp.int32)
    chosen = jnp.where(order == 1, jnp.int32(STEPS - 1), chosen)
    return jnp.where(order == 0, jnp.int32(0), chosen).astype(jnp.int32)


def block_scale(own_key, dims, pieces, low, largest):
    loudness = 1.0
    for position, parts in pieces:
        steps = jax.random.uniform(jax.random.fold_in(jax.random.fold_in(own_key, 6), position), (parts,), jnp.float32, low / len(pieces), largest / len(pieces))
        loudness = loudness * jnp.repeat(jnp.exp(steps), dims[position] // parts).reshape((-1,) + (1,) * (len(dims) - 1 - position))
    return loudness


def centred(key, dims, spread, reach, pieces=(), kind=jnp.bfloat16):
    drawn = spread * jax.random.normal(key, dims, jnp.float32)
    if pieces:
        drawn = drawn * block_scale(key, dims, pieces, -0.22, 0.18)
    return jnp.clip(drawn, -reach, reach).astype(kind)


def setup_inputs(seed: int = 0) -> dict:
    streams_of = jax.random.split(jax.random.key(seed), 9)
    trajectory = centred(streams_of[0], (STEPS, SEQS, SEQUENCE_TOKENS, D), 1.0, 6.0, ((0, 32), (2, 8)), jnp.float32)
    timesteps = draw_timesteps(jax.random.fold_in(streams_of[8], 71), 0)
    offset = draw_offset(jax.random.fold_in(streams_of[8], 71), 0)
    mod_table = centred(streams_of[3], (TOTAL, 3, D), 1.0, 4.0, (), jnp.float32)
    w_qkv = centred(streams_of[4], (D, 3 * HEADS * HEAD_DIM), D ** -0.5, 0.109375, ((0, 32), (1, 8)))
    w_out = centred(streams_of[5], (HEADS * HEAD_DIM, D), (HEADS * HEAD_DIM // 4) ** -0.5, 0.25, ((0, 8), (1, 32)))
    query_gain = jnp.clip(jnp.exp(jax.random.uniform(streams_of[6], (HEAD_DIM,), jnp.float32, math.log(1.0), math.log(3.0))), 1.0, 3.0)
    k_gain = jnp.clip(jnp.exp(jax.random.uniform(streams_of[7], (HEAD_DIM,), jnp.float32, math.log(1.0), math.log(3.0))), 1.0, 3.0)
    return dict(trajectory=trajectory, timesteps=timesteps, offset=offset, mod_table=mod_table, w_qkv=w_qkv, w_out=w_out, query_gain=query_gain, k_gain=k_gain)


eps = 1e-06

def normalize(values):
    mean = lax.optimization_barrier(jnp.mean(values, axis=-1, keepdims=True))
    centered = values - mean
    variance = lax.optimization_barrier(jnp.mean(centered * centered, axis=-1, keepdims=True))
    return centered * lax.rsqrt(variance + eps)

def rms_norm(values):
    return values * lax.rsqrt(lax.optimization_barrier(jnp.mean(values * values, axis=-1, keepdims=True)) + eps)

def block_velocity(current, t_now, mod_table, w_qkv, w_out, query_gain, k_gain):
    modulation = mod_table[t_now]
    hidden = (normalize(current) * (1.0 + modulation[1]) + modulation[0]).astype(jnp.bfloat16)
    qkv = jnp.dot(hidden.reshape(SEQS * SEQUENCE_TOKENS, D), w_qkv, preferred_element_type=jnp.float32)
    qkv = qkv.reshape(SEQS, SEQUENCE_TOKENS, HEADS, 3, HEAD_DIM)
    queries = (rms_norm(qkv[:, :, :, 0, :]) * query_gain).astype(jnp.bfloat16)
    keys = (rms_norm(qkv[:, :, :, 1, :]) * k_gain).astype(jnp.bfloat16)
    values = qkv[:, :, :, 2, :].astype(jnp.bfloat16)
    scores = jnp.einsum('sqhd,skhd->shqk', queries.astype(jnp.float32), keys.astype(jnp.float32)) / math.sqrt(HEAD_DIM)
    weights = jax.nn.softmax(scores, axis=-1).astype(jnp.bfloat16)
    attended = jnp.einsum('shqk,skhd->sqhd', weights.astype(jnp.float32), values.astype(jnp.float32))
    attended = attended.astype(jnp.bfloat16).reshape(SEQS * SEQUENCE_TOKENS, HEADS * HEAD_DIM)
    projected_rows = jnp.dot(attended, w_out, preferred_element_type=jnp.float32).reshape(SEQS, SEQUENCE_TOKENS, D)
    return current + modulation[2] * projected_rows

def reference(trajectory, timesteps, offset, mod_table, w_qkv, w_out, query_gain, k_gain):

    def one_step(index):
        current = trajectory[index]
        drift = block_velocity(current, timesteps[index], mod_table, w_qkv, w_out, query_gain, k_gain)
        step_size = (timesteps[index] - timesteps[index + 1]).astype(jnp.float32) / TOTAL
        return step_size * drift
    indices = jnp.arange(STEPS, dtype=jnp.int32)
    increments = lax.map(one_step, indices)
    live = (indices[:, None] >= offset[None, :])[:, :, None, None]
    terms = jnp.where(live, increments, jnp.float32(0.0))
    prefix = jnp.cumsum(terms, axis=0)
    anchor = trajectory[offset, jnp.arange(SEQS, dtype=jnp.int32)]
    before = (indices[:, None] < offset[None, :])[:, :, None, None]
    return jnp.where(before, trajectory + increments, anchor[None] + prefix)
```

```python
import math

import jax
import jax.numpy as jnp
import numpy as np
from jax import lax
from jax.experimental import pallas as pl
from jax.experimental.pallas import tpu as pltpu
from jax.sharding import Mesh, PartitionSpec as P

eps = 1e-06
AXES = ("y", "x", "h", "z", "c")
NY, NX, NH, NZ, NC = 4, 4, 2, 4, 2
D = 3072
SEQS = 4
ROWS = 32
HEAD = 128
COLS = D // (NX * NC)
TS = 4
BF = jnp.bfloat16
F32 = jnp.float32
VMEM_LIMIT = 48 * 1024 * 1024


def flat(y, x, h, z, c):
    return (((y * NX + x) * NH + h) * NZ + z) * NC + c


def every():
    for y in range(NY):
        for x in range(NX):
            for h in range(NH):
                for z in range(NZ):
                    for c in range(NC):
                        yield y, x, h, z, c


SWAP_XZ = [(flat(*d), flat(d[0], d[3], d[2], d[1], d[4])) for d in every()]
SWAP_YX = [(flat(*d), flat(d[1], d[0], d[2], d[3], d[4])) for d in every()]


def spread(v, axes, parts):
    copies = jnp.broadcast_to(v[None], (parts,) + v.shape)
    return lax.all_to_all(copies, axes, 0, 0)


def other_core(v):
    return lax.ppermute(v, "c", [(0, 1), (1, 0)])


def call(kernel, out_shape, **rest):
    return pl.pallas_call(
        kernel,
        out_shape=out_shape,
        compiler_params=pltpu.CompilerParams(vmem_limit_bytes=VMEM_LIMIT),
        **rest,
    )


def enter_kernel(cur_ref, mod_ref, hidden_ref, state_ref):
    values = cur_ref[0]
    mean = jnp.mean(values, axis=-1, keepdims=True)
    centered = values - mean
    variance = jnp.mean(centered * centered, axis=-1, keepdims=True)
    normal = centered * lax.rsqrt(variance + eps)
    hidden = normal * (1.0 + mod_ref[1:2, :]) + mod_ref[0:1, :]
    hidden_ref[0] = hidden.astype(BF)
    for x in range(NX):
        for c in range(NC):
            at = (x * NC + c) * COLS
            state_ref[x, 0, c] = values[:, at : at + COLS].astype(BF)


def enter(cur, mod):
    return call(
        enter_kernel,
        (
            jax.ShapeDtypeStruct((SEQS, ROWS, D), BF),
            jax.ShapeDtypeStruct((NX, SEQS, NC, ROWS, COLS), BF),
        ),
        grid=(SEQS,),
        in_specs=[
            pl.BlockSpec((1, ROWS, D), lambda s: (s, 0, 0)),
            pl.BlockSpec((3, D), lambda s: (0, 0)),
        ],
        out_specs=(
            pl.BlockSpec((1, ROWS, D), lambda s: (s, 0, 0)),
            pl.BlockSpec((NX, 1, NC, ROWS, COLS), lambda s: (0, s, 0, 0, 0)),
        ),
    )(cur, mod)


def dot(a, b):
    return lax.dot_general(a, b, (((1,), (0,)), ((), ())), preferred_element_type=F32)


def dot_t(a, b):
    return lax.dot_general(a, b, (((1,), (1,)), ((), ())), preferred_element_type=F32)


def rms(values, gain):
    scale = lax.rsqrt(jnp.mean(values * values, axis=-1, keepdims=True) + eps)
    return (values * scale * gain).astype(BF)


def attend_kernel(mine_ref, other_ref, wa_ref, wb_ref, qg_ref, kg_ref, att_ref):
    count, rows = mine_ref.shape[0], mine_ref.shape[1]
    halves = []
    for ref in (mine_ref, other_ref):
        tokens = ref[...].reshape(count * rows, D)
        halves.append((dot(tokens, wa_ref[...]), dot(tokens, wb_ref[...])))

    def part(index, column):
        side = 0 if column < 4 else 1
        at = (column - 4 * side) * HEAD
        here = slice(index * rows, (index + 1) * rows)
        return jnp.concatenate([half[side][here, at : at + HEAD] for half in halves], 0)

    for index in range(count):
        for head in range(2):
            queries = rms(part(index, 3 * head), qg_ref[...])
            keys = rms(part(index, 3 * head + 1), kg_ref[...])
            values = part(index, 3 * head + 2).astype(BF)
            scores = dot_t(queries, keys) * (1.0 / math.sqrt(HEAD))
            scores = jnp.exp(scores - jnp.max(scores, axis=-1, keepdims=True))
            weights = scores / jnp.sum(scores, axis=-1, keepdims=True)
            result = dot(weights.astype(BF), values).astype(BF)
            at = head * HEAD
            att_ref[0, index, :, at : at + HEAD] = result[:rows]
            att_ref[1, index, :, at : at + HEAD] = result[rows:]


def attend(mine, other, wa, wb, qg, kg):
    rows = NZ * ROWS
    step = 2
    whole = lambda *shape: pl.BlockSpec(shape, lambda i: (0,) * len(shape))
    return call(
        attend_kernel,
        jax.ShapeDtypeStruct((2, TS, rows, 2 * HEAD), BF),
        grid=(TS // step,),
        in_specs=[
            pl.BlockSpec((step, rows, D), lambda i: (i, 0, 0)),
            pl.BlockSpec((step, rows, D), lambda i: (i, 0, 0)),
            whole(D, 4 * HEAD),
            whole(D, 2 * HEAD),
            whole(1, HEAD),
            whole(1, HEAD),
        ],
        out_specs=pl.BlockSpec((2, step, rows, 2 * HEAD), lambda i: (0, i, 0, 0)),
    )(mine, other, wa, wb, qg, kg)


def project_kernel(
    ints_ref, floats_ref, att_ref, sib_ref, wm_ref, ws_ref, state_ref, gate_ref, perm_ref, out_ref
):
    rows = NZ * ROWS
    core = ints_ref[0]
    for half in range(2):
        total = None
        for group in range(NX):
            a = att_ref[group, half].reshape(TS * rows, 2 * HEAD)
            b = sib_ref[group, 1 - half].reshape(TS * rows, 2 * HEAD)
            term = dot_t(a, wm_ref[group]) + dot_t(b, ws_ref[group])
            total = term if total is None else total + term
        token_core = core if half == 0 else 1 - core
        values = []
        for t in range(TS):
            projected = total[t * rows : (t + 1) * rows]
            state = state_ref[t, :, token_core].reshape(rows, COLS).astype(F32)
            step, first = floats_ref[t], floats_ref[TS + t]
            increment = step * (state + gate_ref[t : t + 1, :] * projected)
            values.append((increment + first * state).astype(BF).reshape(NZ, ROWS, COLS))
        for z in range(NZ):
            block = jnp.concatenate([v[z] for v in values], 0)
            moved = dot(perm_ref[...], block).astype(BF)
            out_ref[:, z, token_core] = moved.reshape(NY * NH, TS * 4, COLS)


def prefix_kernel(lower_ref, terms_ref, out_ref):
    for c in range(NC):
        terms = terms_ref[:, c].reshape(NY * NH * SEQS * 16, COLS)
        total = dot(lower_ref[...], terms).astype(BF)
        out_ref[:, :, c * COLS : (c + 1) * COLS] = total.reshape(32, 16, COLS)


def leave_kernel(early_ref, got_ref, cur_ref, perm_ref, out_ref):
    got = got_ref[:, 0].reshape(NY * NH * 16, 2 * COLS)
    total = dot(perm_ref[...], got).reshape(SEQS, ROWS, 2 * COLS)
    for s in range(SEQS):
        out_ref[0, s] = total[s] + jnp.where(early_ref[s] > 0, cur_ref[0, s], 0.0)


def row_orders():
    out = np.zeros((128, 128), np.float32)
    back = np.zeros((128, 128), np.float32)
    for part in range(8):
        for a in range(4):
            for t in range(4):
                out[part * 16 + a * 4 + t, a * 32 + part * 4 + t] = 1
                back[a * 32 + part * 4 + t, part * 16 + a * 4 + t] = 1
    return jnp.asarray(out, BF), jnp.asarray(back, BF)


def lower_matrix(offset):
    row, col = np.arange(512), np.arange(512)
    k, s, t = row // 16, (row // 4) % 4, row % 4
    y, h, s2, x, t2 = col // 128, (col // 64) % 2, (col // 16) % 4, (col // 4) % 4, col % 4
    j = (y * NX + x) * NH + h
    same = (s[:, None] == s2[None]) & (t[:, None] == t2[None])
    start = jnp.tile(jnp.repeat(offset, 4), 32)[:, None]
    kk, jj = jnp.asarray(k)[:, None], jnp.asarray(j)[None]
    late = (jj >= start) & (jj <= kk)
    taken = jnp.where(kk >= start, late, jj == kk)
    return (taken & jnp.asarray(same)).astype(BF)


def body(trajectory, timesteps, offset, mod_table, w_qkv, w_out, query_gain, k_gain):
    y, x, h, z, c = (lax.axis_index(a) for a in AXES)
    total = mod_table.shape[0]
    step_of = lambda index: lax.dynamic_index_in_dim(timesteps, index, 0, keepdims=False)
    row_of = lambda index: lax.dynamic_index_in_dim(mod_table, step_of(index), 0, keepdims=False)
    mine = (y * NX + x) * NH + h

    wq = lax.ppermute(w_qkv, AXES, SWAP_XZ)
    hidden, state = enter(trajectory[0], row_of(mine))
    tokens = lax.all_to_all(hidden, "z", 0, 0)

    wa = spread(wq[:, : 4 * HEAD], ("z", "h"), NZ * NH).reshape(-1, 4 * HEAD)
    wa = spread(wa, "y", NY).reshape(D, 4 * HEAD)
    wb = spread(wq[:, 4 * HEAD :], "y", NY)
    wb = lax.all_gather(wb, ("z", "h"), axis=1).reshape(D, 2 * HEAD)

    gathered = spread(tokens.reshape(NZ * ROWS, D), "x", NX)
    other = other_core(gathered)

    state = lax.all_to_all(
        state.reshape(NX * SEQS * NC, ROWS, COLS), ("x", "z", "c"), 0, 0
    ).reshape(NX, NZ, NC, ROWS, COLS)

    wo = lax.ppermute(w_out.T, AXES, SWAP_YX)
    wo = spread(wo, ("z", "h"), NZ * NH).reshape(NZ * NH * 96, 2 * HEAD)
    wo = spread(wo, "y", NY).reshape(NY, NZ, NH, 96, 2 * HEAD)
    pick = lambda core: (
        lax.dynamic_slice_in_dim(wo, 2 * core, 2, 0)
        .transpose(1, 0, 2, 3, 4)
        .reshape(NZ, COLS, 2 * HEAD)
    )
    wo_mine = pick(c)
    wo_other = other_core(pick(1 - c))

    attended = attend(gathered, other, wa, wb, query_gain[None], k_gain[None])
    attended = spread(attended, "x", NX)
    sibling = other_core(attended)

    ks = (y * NX + jnp.arange(TS, dtype=jnp.int32)) * NH + h
    sizes = (timesteps[ks] - timesteps[ks + 1]).astype(F32) / total
    first = (ks == offset[z]).astype(F32)
    gates = lax.dynamic_slice_in_dim(
        jnp.stack([row_of(ks[t])[2] for t in range(TS)]), (x * NC + c) * COLS, COLS, 1
    )
    outward, back = row_orders()
    smem = pl.BlockSpec(memory_space=pltpu.SMEM)
    vmem = pl.BlockSpec(memory_space=pltpu.VMEM)
    terms = call(
        project_kernel,
        jax.ShapeDtypeStruct((NY * NH, NZ, NC, TS * 4, COLS), BF),
        in_specs=[smem, smem] + [vmem] * 7,
        out_specs=vmem,
    )(
        c.astype(jnp.int32)[None],
        jnp.concatenate([sizes, first]),
        attended,
        sibling,
        wo_mine,
        wo_other,
        state,
        gates,
        outward,
    )
    terms = lax.all_to_all(terms.reshape(64, TS * 4, COLS), ("y", "h", "z", "c"), 0, 0)
    sums = call(
        prefix_kernel,
        jax.ShapeDtypeStruct((32, 16, 2 * COLS), BF),
        in_specs=[vmem, vmem],
        out_specs=vmem,
    )(lower_matrix(offset), terms.reshape(32, NC, 16, COLS))
    got = lax.all_to_all(sums, ("y", "x", "h"), 0, 0)
    early = (mine < offset).astype(jnp.int32)
    return call(
        leave_kernel,
        jax.ShapeDtypeStruct((1, SEQS, ROWS, D), F32),
        grid=(NX,),
        in_specs=[
            smem,
            pl.BlockSpec((NY, 1, NH, 16, 2 * COLS), lambda i: (0, i, 0, 0, 0)),
            pl.BlockSpec((1, SEQS, ROWS, 2 * COLS), lambda i: (0, 0, 0, i)),
            pl.BlockSpec((128, 128), lambda i: (0, 0)),
        ],
        out_specs=pl.BlockSpec((1, SEQS, ROWS, 2 * COLS), lambda i: (0, 0, 0, i)),
    )(early, got.reshape(NY, NX, NH, 16, 2 * COLS), trajectory, back)


def solution(mesh):
    fine = Mesh(mesh.devices.reshape(NY, NX, NH, NZ, NC), AXES)
    steps, places = ("y", "x", "h"), ("z", "c")
    return jax.shard_map(
        body,
        mesh=fine,
        in_specs=(
            P(steps, None, places, None),
            P(),
            P(),
            P(),
            P(steps, places),
            P(places, steps),
            P(),
            P(),
        ),
        out_specs=P(steps, None, places, None),
        check_vma=False,
    )
```

```python
import math

import jax
import jax.numpy as jnp
import numpy as np
from jax import lax
from jax.experimental import pallas as pl
from jax.experimental.pallas import tpu as pltpu
from jax.sharding import Mesh, PartitionSpec as P

eps = 1e-06
AXES = ("y", "x", "h", "z", "c")
NY, NX, NH, NZ, NC = 4, 4, 2, 4, 2
D = 3072
SEQS = 4
ROWS = 32
HEAD = 128
COLS = D // (NX * NC)
TS = 4
BF = jnp.bfloat16
F32 = jnp.float32
VMEM_LIMIT = 48 * 1024 * 1024
AWAY = (0, 3, 1, 2)


def flat(y, x, h, z, c):
    return (((y * NX + x) * NH + h) * NZ + z) * NC + c


def every():
    for y in range(NY):
        for x in range(NX):
            for h in range(NH):
                for z in range(NZ):
                    for c in range(NC):
                        yield y, x, h, z, c


SWAP_XZ = [(flat(*d), flat(d[0], d[3], d[2], d[1], d[4])) for d in every()]
SWAP_YX = [(flat(*d), flat(d[1], d[0], d[2], d[3], d[4])) for d in every()]


def spread(v, axes, parts):
    copies = jnp.broadcast_to(v[None], (parts,) + v.shape)
    return lax.all_to_all(copies, axes, 0, 0)


def other_core(v):
    return lax.ppermute(v, "c", [(0, 1), (1, 0)])


def shift(v, axis, size, away):
    return lax.ppermute(v, axis, [(i, (i + away) % size) for i in range(size)])


def ring(v, axis, size, first, second):
    before = shift(v, axis, size, 1)
    after = shift(v, axis, size, -1)
    far = (shift(first(before), axis, size, 1), shift(second(after), axis, size, -1))
    return (v, before, after) + far


def halves(v):
    n = v.shape[0] // 2
    return v[:n], v[n:]


def ring_rows(v, axis, size):
    return ring(v, axis, size, lambda b: halves(b)[0], lambda b: halves(b)[1])


def after(v, other):
    return lax.optimization_barrier((v, other))[0]


def call(kernel, out_shape, **rest):
    return pl.pallas_call(
        kernel,
        out_shape=out_shape,
        compiler_params=pltpu.CompilerParams(vmem_limit_bytes=VMEM_LIMIT),
        **rest,
    )


def enter_kernel(cur_ref, mod_ref, hidden_ref, state_ref):
    values = cur_ref[0]
    mean = jnp.mean(values, axis=-1, keepdims=True)
    centered = values - mean
    variance = jnp.mean(centered * centered, axis=-1, keepdims=True)
    normal = centered * lax.rsqrt(variance + eps)
    hidden = normal * (1.0 + mod_ref[1:2, :]) + mod_ref[0:1, :]
    hidden_ref[0] = hidden.astype(BF)
    for x in range(NX):
        for c in range(NC):
            at = (x * NC + c) * COLS
            state_ref[x, 0, c] = values[:, at : at + COLS].astype(BF)


def enter(cur, mod):
    return call(
        enter_kernel,
        (
            jax.ShapeDtypeStruct((SEQS, ROWS, D), BF),
            jax.ShapeDtypeStruct((NX, SEQS, NC, ROWS, COLS), BF),
        ),
        grid=(SEQS,),
        in_specs=[
            pl.BlockSpec((1, ROWS, D), lambda s: (s, 0, 0)),
            pl.BlockSpec((3, D), lambda s: (0, 0)),
        ],
        out_specs=(
            pl.BlockSpec((1, ROWS, D), lambda s: (s, 0, 0)),
            pl.BlockSpec((NX, 1, NC, ROWS, COLS), lambda s: (0, s, 0, 0, 0)),
        ),
    )(cur, mod)


def dot(a, b):
    return lax.dot_general(a, b, (((1,), (0,)), ((), ())), preferred_element_type=F32)


def dot_t(a, b):
    return lax.dot_general(a, b, (((1,), (1,)), ((), ())), preferred_element_type=F32)


def rms(values, gain):
    scale = lax.rsqrt(jnp.mean(values * values, axis=-1, keepdims=True) + eps)
    return (values * scale * gain).astype(BF)


def attend_kernel(ints_ref, *refs):
    mine, others, weights = refs[0:5], refs[5:10], refs[10:15]
    qg_ref, kg_ref, att_ref, tokens_ref, qkv_ref = refs[15:]
    rows = NZ * ROWS
    half = rows // 2
    for side, pieces in enumerate((mine, others)):
        for place in range(3):
            tokens_ref[side * TS + place] = pieces[place][...]
        tokens_ref[side * TS + 3, :half] = pieces[3][...]
        tokens_ref[side * TS + 3, half:] = pieces[4][...]
    y = ints_ref[0]
    wide = D // NY
    starts = [y * wide]
    for away in (NY - 1, 1):
        starts.append(lax.rem(y + away, NY) * wide)
    starts.append(lax.rem(y + 2, NY) * wide)
    starts.append(starts[3] + wide // 2)
    for place, weight in enumerate(weights):
        depth = weight.shape[0]
        columns = pl.ds(pl.multiple_of(starts[place], HEAD), depth)
        term = dot(tokens_ref[:, :, columns].reshape(2 * TS * rows, depth), weight[...])
        if place == 0:
            qkv_ref[...] = term
        else:
            qkv_ref[...] += term

    def part(index, column):
        at = column * HEAD
        first, second = index * rows, (TS + index) * rows
        return jnp.concatenate(
            [qkv_ref[first : first + rows, at : at + HEAD], qkv_ref[second : second + rows, at : at + HEAD]], 0
        )

    for index in range(TS):
        for head in range(2):
            queries = rms(part(index, 3 * head), qg_ref[...])
            keys = rms(part(index, 3 * head + 1), kg_ref[...])
            values = part(index, 3 * head + 2).astype(BF)
            scores = dot_t(queries, keys) * (1.0 / math.sqrt(HEAD))
            scores = jnp.exp(scores - jnp.max(scores, axis=-1, keepdims=True))
            share = scores / jnp.sum(scores, axis=-1, keepdims=True)
            result = dot(share.astype(BF), values).astype(BF)
            at = head * HEAD
            att_ref[0, index, :, at : at + HEAD] = result[:rows]
            att_ref[1, index, :, at : at + HEAD] = result[rows:]


def attend(y, mine, others, weights, qg, kg):
    rows = NZ * ROWS
    smem = pl.BlockSpec(memory_space=pltpu.SMEM)
    vmem = pl.BlockSpec(memory_space=pltpu.VMEM)
    return call(
        attend_kernel,
        jax.ShapeDtypeStruct((2, TS, rows, 2 * HEAD), BF),
        in_specs=[smem] + [vmem] * 17,
        out_specs=vmem,
        scratch_shapes=[
            pltpu.VMEM((2 * TS, rows, D), BF),
            pltpu.VMEM((2 * TS * rows, 6 * HEAD), F32),
        ],
    )(y[None], *mine, *others, *weights, qg, kg)


def project_kernel(ints_ref, floats_ref, *refs):
    att, sib = refs[0:5], refs[5:10]
    wm_ref, ws_ref, state_ref, gate_ref, perm_ref, out_ref = refs[10:]
    rows = NZ * ROWS
    core, x = ints_ref[0], ints_ref[1]

    def block(pieces, place, half):
        if place < 3:
            return pieces[place][half].reshape(TS * rows, 2 * HEAD)
        return pieces[3 + half][...].reshape(TS * rows, 2 * HEAD)

    for half in range(2):
        totals = [None] * TS
        for place, away in enumerate(AWAY):
            group = lax.rem(x + away, NX)
            a = block(att, place, half)
            b = block(sib, place, 1 - half)
            term = dot_t(a, wm_ref[group]) + dot_t(b, ws_ref[group])
            for j in range(TS):
                at = AWAY.index((j - away) % NX) * rows
                piece = term[at : at + rows]
                totals[j] = piece if totals[j] is None else totals[j] + piece
        token_core = core if half == 0 else 1 - core
        values = []
        for j in range(TS):
            state = state_ref[lax.rem(x + j, NX), :, token_core].reshape(rows, COLS).astype(F32)
            step, first = floats_ref[j], floats_ref[TS + j]
            increment = step * (state + gate_ref[j : j + 1, :] * totals[j])
            values.append((increment + first * state).astype(BF).reshape(NZ, ROWS, COLS))
        for z in range(NZ):
            stacked = jnp.concatenate([v[z] for v in values], 0)
            moved = dot(perm_ref[...], stacked).astype(BF)
            out_ref[:, z, token_core] = moved.reshape(NY * NH, TS * 4, COLS)


def prefix_kernel(lower_ref, terms_ref, out_ref):
    for c in range(NC):
        terms = terms_ref[:, c].reshape(NY * NH * SEQS * 16, COLS)
        total = dot(lower_ref[...], terms).astype(BF)
        out_ref[:, :, c * COLS : (c + 1) * COLS] = total.reshape(32, 16, COLS)


def leave_kernel(early_ref, got_ref, cur_ref, perm_ref, out_ref):
    got = got_ref[:, 0].reshape(NY * NH * 16, 2 * COLS)
    total = dot(perm_ref[...], got).reshape(SEQS, ROWS, 2 * COLS)
    for s in range(SEQS):
        out_ref[0, s] = total[s] + jnp.where(early_ref[s] > 0, cur_ref[0, s], 0.0)


def row_orders():
    out = np.zeros((128, 128), np.float32)
    back = np.zeros((128, 128), np.float32)
    for part in range(8):
        for a in range(4):
            for t in range(4):
                out[part * 16 + a * 4 + t, a * 32 + part * 4 + t] = 1
                back[a * 32 + part * 4 + t, part * 16 + a * 4 + t] = 1
    return jnp.asarray(out, BF), jnp.asarray(back, BF)


def lower_matrix(offset, here):
    row, col = np.arange(512), np.arange(512)
    k, s, t = row // 16, (row // 4) % 4, row % 4
    y, h, s2, x, t2 = col // 128, (col // 64) % 2, (col // 16) % 4, (col // 4) % 4, col % 4
    j = (jnp.asarray(y) * NX + lax.rem(jnp.asarray(x) + here, NX)) * NH + jnp.asarray(h)
    same = (s[:, None] == s2[None]) & (t[:, None] == t2[None])
    start = jnp.tile(jnp.repeat(offset, 4), 32)[:, None]
    kk, jj = jnp.asarray(k)[:, None], j[None]
    late = (jj >= start) & (jj <= kk)
    taken = jnp.where(kk >= start, late, jj == kk)
    return (taken & jnp.asarray(same)).astype(BF)


def body(trajectory, timesteps, offset, mod_table, w_qkv, w_out, query_gain, k_gain):
    y, x, h, z, c = (lax.axis_index(a) for a in AXES)
    total = mod_table.shape[0]
    step_of = lambda index: lax.dynamic_index_in_dim(timesteps, index, 0, keepdims=False)
    row_of = lambda index: lax.dynamic_index_in_dim(mod_table, step_of(index), 0, keepdims=False)
    mine = (y * NX + x) * NH + h

    wq = lax.ppermute(w_qkv, AXES, SWAP_XZ)
    wo = lax.ppermute(w_out.T, AXES, SWAP_YX)
    hidden, state = enter(trajectory[0], row_of(mine))
    tokens = lax.all_to_all(hidden, "z", 0, 0)

    wq = spread(after(wq, tokens), ("z", "h"), NZ * NH).reshape(-1, 6 * HEAD)
    weights = ring_rows(wq, "y", NY)

    tokens = ring_rows(tokens.reshape(NZ * ROWS, D), "x", NX)
    others = [other_core(v) for v in tokens]

    wo = spread(after(wo, wq), ("z", "h"), NZ * NH).reshape(NZ * NH * 96, 2 * HEAD)
    state = lax.all_to_all(
        after(state, wo).reshape(NX * SEQS * NC, ROWS, COLS), ("x", "z", "c"), 0, 0
    ).reshape(NX, NZ, NC, ROWS, COLS)

    attended = attend(after(y, state), tokens, others, weights, query_gain[None], k_gain[None])

    wo = ring_rows(wo, "y", NY)
    wo = jnp.stack(wo[:3] + (jnp.concatenate(wo[3:], 0),))
    wo = wo.reshape(NY, NZ, NH, 96, 2 * HEAD)
    place = jnp.array([AWAY.index(i) for i in range(NY)], jnp.int32)

    def pick(core):
        both = [wo[place[lax.rem(2 * core + i - y + NY, NY)]] for i in range(2)]
        return jnp.stack(both, 1).reshape(NZ, COLS, 2 * HEAD)

    wo_mine = pick(c)
    wo_other = other_core(pick(1 - c))

    attended = ring(attended, "x", NX, lambda b: b[0], lambda b: b[1])
    sibling = [other_core(v) for v in attended]

    ks = (y * NX + lax.rem(x + jnp.arange(TS, dtype=jnp.int32), NX)) * NH + h
    sizes = (timesteps[ks] - timesteps[ks + 1]).astype(F32) / total
    first = (ks == offset[z]).astype(F32)
    gates = lax.dynamic_slice_in_dim(
        jnp.stack([row_of(ks[t])[2] for t in range(TS)]), (x * NC + c) * COLS, COLS, 1
    )
    outward, back = row_orders()
    smem = pl.BlockSpec(memory_space=pltpu.SMEM)
    vmem = pl.BlockSpec(memory_space=pltpu.VMEM)
    terms = call(
        project_kernel,
        jax.ShapeDtypeStruct((NY * NH, NZ, NC, TS * 4, COLS), BF),
        in_specs=[smem, smem] + [vmem] * 15,
        out_specs=vmem,
    )(
        jnp.stack([c, x]).astype(jnp.int32),
        jnp.concatenate([sizes, first]),
        *attended,
        *sibling,
        wo_mine,
        wo_other,
        state,
        gates,
        outward,
    )
    terms = lax.all_to_all(terms.reshape(64, TS * 4, COLS), ("y", "h", "z", "c"), 0, 0)
    sums = call(
        prefix_kernel,
        jax.ShapeDtypeStruct((32, 16, 2 * COLS), BF),
        in_specs=[vmem, vmem],
        out_specs=vmem,
    )(lower_matrix(offset, x), terms.reshape(32, NC, 16, COLS))
    got = lax.all_to_all(sums, ("y", "x", "h"), 0, 0)
    early = (mine < offset).astype(jnp.int32)
    return call(
        leave_kernel,
        jax.ShapeDtypeStruct((1, SEQS, ROWS, D), F32),
        grid=(NX,),
        in_specs=[
            smem,
            pl.BlockSpec((NY, 1, NH, 16, 2 * COLS), lambda i: (0, i, 0, 0, 0)),
            pl.BlockSpec((1, SEQS, ROWS, 2 * COLS), lambda i: (0, 0, 0, i)),
            pl.BlockSpec((128, 128), lambda i: (0, 0)),
        ],
        out_specs=pl.BlockSpec((1, SEQS, ROWS, 2 * COLS), lambda i: (0, 0, 0, i)),
    )(early, got.reshape(NY, NX, NH, 16, 2 * COLS), trajectory, back)


def solution(mesh):
    fine = Mesh(mesh.devices.reshape(NY, NX, NH, NZ, NC), AXES)
    steps, places = ("y", "x", "h"), ("z", "c")
    return jax.shard_map(
        body,
        mesh=fine,
        in_specs=(
            P(steps, None, places, None),
            P(),
            P(),
            P(),
            P(steps, places),
            P(places, steps),
            P(),
            P(),
        ),
        out_specs=P(steps, None, places, None),
        check_vma=False,
    )
```

```python
import math

import jax
import jax.numpy as jnp
import numpy as np
from jax import lax
from jax.experimental import pallas as pl
from jax.experimental.pallas import tpu as pltpu
from jax.sharding import Mesh, PartitionSpec as P

eps = 1e-06
AXES = ("y", "x", "h", "z", "c")
NY, NX, NH, NZ, NC = 4, 4, 2, 4, 2
D = 3072
SEQS = 4
ROWS = 32
HEAD = 128
COLS = D // (NX * NC)
TS = 4
WIDE = D // NY
TOKENS = NZ * ROWS
AWAY = (0, 3, 1, 2)
BF = jnp.bfloat16
F32 = jnp.float32
VMEM_LIMIT = 48 * 1024 * 1024
SMEM = pl.BlockSpec(memory_space=pltpu.SMEM)
VMEM = pl.BlockSpec(memory_space=pltpu.VMEM)


def flat(y, x, h, z, c):
    return (((y * NX + x) * NH + h) * NZ + z) * NC + c


def every():
    for y in range(NY):
        for x in range(NX):
            for h in range(NH):
                for z in range(NZ):
                    for c in range(NC):
                        yield y, x, h, z, c


TO_HEADS = [(flat(y, x, h, z, c), flat(y, z, h, x, c)) for y, x, h, z, c in every()]
TO_COLUMNS = [
    (flat(y, x, h, z, c), flat((x % 2) * 2 + c, y, h, z, x // 2)) for y, x, h, z, c in every()
]


def spread(v, axes, parts):
    copies = jnp.broadcast_to(v[None], (parts,) + v.shape)
    return lax.all_to_all(copies, axes, 0, 0)


def other_core(v):
    return lax.ppermute(v, "c", [(0, 1), (1, 0)])


def shift(v, axis, size, away):
    return lax.ppermute(v, axis, [(i, (i + away) % size) for i in range(size)])


def ring(v, axis, size, first, second):
    before = shift(v, axis, size, 1)
    after_ = shift(v, axis, size, -1)
    far = (shift(first(before), axis, size, 1), shift(second(after_), axis, size, -1))
    return (v, before, after_) + far


def ring_rows(v, axis, size):
    n = v.shape[0] // 2
    return ring(v, axis, size, lambda b: b[:n], lambda b: b[n:])


def after(v, other):
    return lax.optimization_barrier((v, other))[0]


def call(kernel, out_shape, specs, **rest):
    return pl.pallas_call(
        kernel,
        out_shape=out_shape,
        in_specs=specs,
        compiler_params=pltpu.CompilerParams(vmem_limit_bytes=VMEM_LIMIT),
        **rest,
    )


def dot(a, b):
    return lax.dot_general(a, b, (((1,), (0,)), ((), ())), preferred_element_type=F32)


def dot_t(a, b):
    return lax.dot_general(a, b, (((1,), (1,)), ((), ())), preferred_element_type=F32)


def step_index(y, x, h):
    return (y * NX + x) * NH + h


def my_step():
    return step_index(lax.axis_index("y"), lax.axis_index("x"), lax.axis_index("h"))


def enter_kernel(steps_ref, cur_ref, mod_ref, hidden_ref, state_ref):
    now = steps_ref[my_step()]
    shift_row = mod_ref[0, pl.ds(now, 1), :]
    scale_row = 1.0 + mod_ref[1, pl.ds(now, 1), :]
    for s in range(SEQS):
        values = cur_ref[0, s]
        mean = jnp.mean(values, axis=-1, keepdims=True)
        centered = values - mean
        variance = jnp.mean(centered * centered, axis=-1, keepdims=True)
        normal = centered * lax.rsqrt(variance + eps)
        hidden_ref[s] = (normal * scale_row + shift_row).astype(BF)
        for x in range(NX):
            for c in range(NC):
                at = (x * NC + c) * COLS
                state_ref[x, s, c] = values[:, at : at + COLS].astype(BF)


def lower_kernel(offset_ref, out_ref):
    shape = (512, 512)
    row = lax.broadcasted_iota(jnp.int32, shape, 0)
    col = lax.broadcasted_iota(jnp.int32, shape, 1)
    bits = lambda v, at, n: (v >> at) & ((1 << n) - 1)
    k, s, t = row >> 4, bits(row, 2, 2), bits(row, 0, 2)
    y, h, s2 = col >> 7, bits(col, 6, 1), bits(col, 4, 2)
    x = (bits(col, 2, 2) + lax.axis_index("x")) & (NX - 1)
    j = step_index(y, x, h)
    start = jnp.full(shape, offset_ref[0], jnp.int32)
    for index in range(1, SEQS):
        start = jnp.where(s == index, offset_ref[index], start)
    same = (s == s2) & (t == bits(col, 0, 2))
    late = (k >= start) & (j >= start) & (j <= k)
    alone = (k < start) & (j == k)
    out_ref[...] = jnp.where(same & (late | alone), 1.0, 0.0).astype(BF)


def rms(values, gain):
    scale = lax.rsqrt(jnp.mean(values * values, axis=-1, keepdims=True) + eps)
    return (values * scale * gain).astype(BF)


def fill_tokens(tokens_ref, pieces):
    half = TOKENS // 2
    for side in range(2):
        mine = pieces[5 * side : 5 * side + 5]
        for place in range(3):
            tokens_ref[side * TS + place] = mine[place][...]
        tokens_ref[side * TS + 3, :half] = mine[3][...]
        tokens_ref[side * TS + 3, half:] = mine[4][...]


def product(tokens_ref, weight, start):
    depth = weight.shape[0]
    columns = pl.ds(pl.multiple_of(start, HEAD), depth)
    return dot(tokens_ref[:, :, columns].reshape(2 * TS * TOKENS, depth), weight[...])


def qkv_kernel(*refs):
    weights, (qkv_ref, tokens_ref) = refs[10:13], refs[13:]
    fill_tokens(tokens_ref, refs[:10])
    y = lax.axis_index("y")
    for place, weight in enumerate(weights):
        term = product(tokens_ref, weight, lax.rem(y + AWAY[place], NY) * WIDE)
        if place == 0:
            qkv_ref[...] = term
        else:
            qkv_ref[...] += term


def attend_kernel(*refs):
    weights = refs[10:12]
    partial_ref, qg_ref, kg_ref, att_ref, tokens_ref, qkv_ref = refs[12:]
    fill_tokens(tokens_ref, refs[:10])
    start = lax.rem(lax.axis_index("y") + 2, NY) * WIDE
    qkv_ref[...] = partial_ref[...] + product(tokens_ref, weights[0], start)
    qkv_ref[...] += product(tokens_ref, weights[1], start + WIDE // 2)

    def part(index, column):
        here = slice(column * HEAD, (column + 1) * HEAD)
        first, second = index * TOKENS, (TS + index) * TOKENS
        return jnp.concatenate(
            [qkv_ref[first : first + TOKENS, here], qkv_ref[second : second + TOKENS, here]], 0
        )

    for index in range(TS):
        for head in range(2):
            queries = rms(part(index, 3 * head), qg_ref[...])
            keys = rms(part(index, 3 * head + 1), kg_ref[...])
            values = part(index, 3 * head + 2).astype(BF)
            scores = dot_t(queries, keys) * (1.0 / math.sqrt(HEAD))
            scores = jnp.exp(scores - jnp.max(scores, axis=-1, keepdims=True))
            share = scores / jnp.sum(scores, axis=-1, keepdims=True)
            result = dot(share.astype(BF), values).astype(BF)
            at = head * HEAD
            att_ref[0, index, :, at : at + HEAD] = result[:TOKENS]
            att_ref[1, index, :, at : at + HEAD] = result[TOKENS:]


def project_kernel(steps_ref, offset_ref, mod_ref, *refs):
    att, sib, blocks = refs[0:5], refs[5:10], refs[10:15]
    state_ref, perm_ref, out_ref, weight_ref = refs[15:]
    y, x, h, z, core = (lax.axis_index(a) for a in AXES)
    plans = mod_ref.shape[1]

    for place, block in enumerate(blocks):
        source = lax.rem(y + AWAY[min(place, 3)], NY)
        into = lax.rem(source, 2)
        down = pl.multiple_of((source >> 1) * (COLS // 2), 16)
        zs = {3: (0, 1), 4: (2, 3)}.get(place, range(NZ))
        for at, zz in enumerate(zs):
            rows = COLS // 2
            weight_ref[into, zz, pl.ds(down, rows)] = block[at * rows : (at + 1) * rows]

    def piece(pieces, place, half):
        if place < 3:
            return pieces[place][half].reshape(TS * TOKENS, 2 * HEAD)
        return pieces[3 + half][...].reshape(TS * TOKENS, 2 * HEAD)

    column = pl.multiple_of((x * NC + core) * COLS, HEAD)
    for half in range(2):
        totals = [None] * TS
        for place, away in enumerate(AWAY):
            group = lax.rem(x + away, NX)
            term = dot_t(piece(att, place, half), weight_ref[core, group])
            term += dot_t(piece(sib, place, 1 - half), weight_ref[1 - core, group])
            for j in range(TS):
                at = AWAY.index((j - away) % NX) * TOKENS
                rows = term[at : at + TOKENS]
                totals[j] = rows if totals[j] is None else totals[j] + rows
        token_core = core if half == 0 else 1 - core
        values = []
        for j in range(TS):
            there = lax.rem(x + j, NX)
            k = step_index(y, there, h)
            now = steps_ref[k]
            size = (now - steps_ref[k + 1]).astype(F32) / plans
            first = jnp.where(k == offset_ref[z], 1.0, 0.0)
            gate = mod_ref[2, pl.ds(now, 1), pl.ds(column, COLS)]
            state = state_ref[there, :, token_core].reshape(TOKENS, COLS).astype(F32)
            increment = size * (state + gate * totals[j])
            values.append((increment + first * state).astype(BF).reshape(NZ, ROWS, COLS))
        for zz in range(NZ):
            stacked = jnp.concatenate([v[zz] for v in values], 0)
            moved = dot(perm_ref[...], stacked).astype(BF)
            out_ref[:, zz, token_core] = moved.reshape(NY * NH, TS * 4, COLS)


def prefix_kernel(lower_ref, terms_ref, out_ref):
    for c in range(NC):
        terms = terms_ref[:, c].reshape(NY * NH * SEQS * 16, COLS)
        total = dot(lower_ref[...], terms).astype(BF)
        out_ref[:, :, c * COLS : (c + 1) * COLS] = total.reshape(32, 16, COLS)


def leave_kernel(offset_ref, got_ref, cur_ref, perm_ref, out_ref):
    got = got_ref[:, 0].reshape(NY * NH * 16, 2 * COLS)
    total = dot(perm_ref[...], got).reshape(SEQS, ROWS, 2 * COLS)
    mine = my_step()
    for s in range(SEQS):
        out_ref[0, s] = total[s] + jnp.where(mine < offset_ref[s], cur_ref[0, s], 0.0)


def row_orders():
    out = np.zeros((128, 128), np.float32)
    for part in range(8):
        for a in range(4):
            for t in range(4):
                out[part * 16 + a * 4 + t, a * 32 + part * 4 + t] = 1
    return jnp.asarray(out, BF), jnp.asarray(out.T, BF)


def shape(*dims, kind=BF):
    return jax.ShapeDtypeStruct(dims, kind)


def body(trajectory, timesteps, offset, mod_table, w_qkv, w_out, query_gain, k_gain):
    planes = mod_table.transpose(1, 0, 2)
    wq = lax.ppermute(w_qkv, AXES, TO_HEADS)
    wo = lax.ppermute(w_out.T, AXES, TO_COLUMNS)
    hidden, state = call(
        enter_kernel,
        (shape(SEQS, ROWS, D), shape(NX, SEQS, NC, ROWS, COLS)),
        [SMEM, VMEM, VMEM],
        out_specs=(VMEM, VMEM),
    )(timesteps, trajectory, planes)
    lower = call(lower_kernel, shape(512, 512), [SMEM], out_specs=VMEM)(offset)

    tokens = lax.all_to_all(hidden, "z", 0, 0)
    wq = spread(after(wq, tokens), ("z", "h"), NZ * NH).reshape(WIDE, 6 * HEAD)
    weights = ring_rows(wq, "y", NY)
    tokens = ring_rows(tokens.reshape(TOKENS, D), "x", NX)
    others = tuple(other_core(v) for v in tokens)

    wo = spread(after(wo, wq), ("z", "h"), NZ * NH).reshape(NZ * NH * 96, 2 * HEAD)
    state = lax.all_to_all(
        after(state, (wo, tokens[3], tokens[4])).reshape(NX * SEQS * NC, ROWS, COLS), ("x", "z", "c"), 0, 0
    ).reshape(NX, NZ, NC, ROWS, COLS)
    columns = ring_rows(wo, "y", NY)

    scratch = [pltpu.VMEM((2 * TS, TOKENS, D), BF)]
    partial = call(
        qkv_kernel,
        shape(2 * TS * TOKENS, 6 * HEAD, kind=F32),
        [VMEM] * 13,
        out_specs=VMEM,
        scratch_shapes=scratch,
    )(*tokens, *others, *weights[:3])
    attended = call(
        attend_kernel,
        shape(2, TS, TOKENS, 2 * HEAD),
        [VMEM] * 15,
        out_specs=VMEM,
        scratch_shapes=scratch + [pltpu.VMEM((2 * TS * TOKENS, 6 * HEAD), F32)],
    )(*tokens, *others, *weights[3:], partial, query_gain[None], k_gain[None])

    attended = ring(after(attended, state), "x", NX, lambda b: b[0], lambda b: b[1])
    sibling = tuple(other_core(v) for v in attended)

    outward, back = row_orders()
    terms = call(
        project_kernel,
        shape(NY * NH, NZ, NC, TS * 4, COLS),
        [SMEM, SMEM] + [VMEM] * 18,
        out_specs=VMEM,
        scratch_shapes=[pltpu.VMEM((NC, NZ, COLS, 2 * HEAD), BF)],
    )(timesteps, offset, planes, *attended, *sibling, *columns, state, outward)
    terms = lax.all_to_all(terms.reshape(64, TS * 4, COLS), ("y", "h", "z", "c"), 0, 0)
    sums = call(prefix_kernel, shape(32, 16, 2 * COLS), [VMEM, VMEM], out_specs=VMEM)(
        lower, terms.reshape(32, NC, 16, COLS)
    )
    got = lax.all_to_all(sums, ("y", "x", "h"), 0, 0)
    return call(
        leave_kernel,
        shape(1, SEQS, ROWS, D, kind=F32),
        [
            SMEM,
            pl.BlockSpec((NY, 1, NH, 16, 2 * COLS), lambda i: (0, i, 0, 0, 0)),
            pl.BlockSpec((1, SEQS, ROWS, 2 * COLS), lambda i: (0, 0, 0, i)),
            pl.BlockSpec((128, 128), lambda i: (0, 0)),
        ],
        grid=(NX,),
        out_specs=pl.BlockSpec((1, SEQS, ROWS, 2 * COLS), lambda i: (0, 0, 0, i)),
    )(offset, got.reshape(NY, NX, NH, 16, 2 * COLS), trajectory, back)


def solution(mesh):
    fine = Mesh(mesh.devices.reshape(NY, NX, NH, NZ, NC), AXES)
    steps, places = ("y", "x", "h"), ("z", "c")
    return jax.shard_map(
        body,
        mesh=fine,
        in_specs=(
            P(steps, None, places, None),
            P(),
            P(),
            P(),
            P(steps, places),
            P(places, steps),
            P(),
            P(),
        ),
        out_specs=P(steps, None, places, None),
        check_vma=False,
    )
```

```python
import math

import jax
import jax.numpy as jnp
import numpy as np
from jax import lax
from jax.experimental import pallas as pl
from jax.experimental.pallas import tpu as pltpu
from jax.sharding import Mesh, PartitionSpec as P

eps = 1e-06
AXES = ("y", "x", "h", "z", "c")
NY, NX, NH, NZ, NC = 4, 4, 2, 4, 2
D = 3072
SEQS = 4
ROWS = 32
HEAD = 128
COLS = D // (NX * NC)
TS = 4
WIDE = D // NY
TOKENS = NZ * ROWS
AWAY = (0, 3, 1, 2)
BF = jnp.bfloat16
F32 = jnp.float32
SMEM = pl.BlockSpec(memory_space=pltpu.SMEM)
VMEM = pl.BlockSpec(memory_space=pltpu.VMEM)
HBM = pl.BlockSpec(memory_space=pltpu.HBM)


def flat(y, x, h, z, c):
    return (((y * NX + x) * NH + h) * NZ + z) * NC + c


def every():
    for y in range(NY):
        for x in range(NX):
            for h in range(NH):
                for z in range(NZ):
                    for c in range(NC):
                        yield y, x, h, z, c


TO_HEADS = [(flat(y, x, h, z, c), flat(y, z, h, x, c)) for y, x, h, z, c in every()]
TO_COLUMNS = [
    (flat(y, x, h, z, c), flat((x % 2) * 2 + c, y, h, z, x // 2)) for y, x, h, z, c in every()
]


def spread(v, axes, parts):
    copies = jnp.broadcast_to(v[None], (parts,) + v.shape)
    return lax.all_to_all(copies, axes, 0, 0)


def other_core(v):
    return lax.ppermute(v, "c", [(0, 1), (1, 0)])


def shift(v, axis, size, away):
    return lax.ppermute(v, axis, [(i, (i + away) % size) for i in range(size)])


def ring(v, axis, size, first, second):
    before = shift(v, axis, size, 1)
    after_ = shift(v, axis, size, -1)
    far = (shift(first(before), axis, size, 1), shift(second(after_), axis, size, -1))
    return (v, before, after_) + far


def ring_rows(v, axis, size):
    n = v.shape[0] // 2
    return ring(v, axis, size, lambda b: b[:n], lambda b: b[n:])


def after(v, other):
    return lax.optimization_barrier((v, other))[0]


def call(kernel, out_shape, specs, mib=48, **rest):
    return pl.pallas_call(
        kernel,
        out_shape=out_shape,
        in_specs=specs,
        compiler_params=pltpu.CompilerParams(vmem_limit_bytes=mib * 1024 * 1024),
        **rest,
    )


def dot(a, b):
    return lax.dot_general(a, b, (((1,), (0,)), ((), ())), preferred_element_type=F32)


def dot_t(a, b):
    return lax.dot_general(a, b, (((1,), (1,)), ((), ())), preferred_element_type=F32)


def step_index(y, x, h):
    return (y * NX + x) * NH + h


def my_step():
    return step_index(lax.axis_index("y"), lax.axis_index("x"), lax.axis_index("h"))


def enter_kernel(steps_ref, cur_hbm, mod_hbm, hidden_ref, state_ref, cur_ref, mod_ref, sems):
    plane = pltpu.make_async_copy(mod_hbm.at[0:2], mod_ref, sems.at[SEQS])
    loads = [
        pltpu.make_async_copy(cur_hbm.at[0, s], cur_ref.at[s], sems.at[s]) for s in range(SEQS)
    ]
    for copy in loads + [plane]:
        copy.start()
    now = steps_ref[my_step()]
    for s in range(SEQS):
        loads[s].wait()
        values = cur_ref[s]
        mean = jnp.mean(values, axis=-1, keepdims=True)
        centered = values - mean
        variance = jnp.mean(centered * centered, axis=-1, keepdims=True)
        cur_ref[s] = centered * lax.rsqrt(variance + eps)
        for x in range(NX):
            for c in range(NC):
                at = (x * NC + c) * COLS
                state_ref[x, s, c] = values[:, at : at + COLS].astype(BF)
    plane.wait()
    shift_row = mod_ref[0, pl.ds(now, 1), :]
    scale_row = 1.0 + mod_ref[1, pl.ds(now, 1), :]
    for s in range(SEQS):
        hidden_ref[s] = (cur_ref[s] * scale_row + shift_row).astype(BF)


def lower_kernel(offset_ref, out_ref):
    shape = (512, 512)
    row = lax.broadcasted_iota(jnp.int32, shape, 0)
    col = lax.broadcasted_iota(jnp.int32, shape, 1)
    bits = lambda v, at, n: (v >> at) & ((1 << n) - 1)
    k, s, t = row >> 4, bits(row, 2, 2), bits(row, 0, 2)
    y, h, s2 = col >> 7, bits(col, 6, 1), bits(col, 4, 2)
    x = (bits(col, 2, 2) + lax.axis_index("x")) & (NX - 1)
    j = step_index(y, x, h)
    start = jnp.full(shape, offset_ref[0], jnp.int32)
    for index in range(1, SEQS):
        start = jnp.where(s == index, offset_ref[index], start)
    same = (s == s2) & (t == bits(col, 0, 2))
    late = (k >= start) & (j >= start) & (j <= k)
    alone = (k < start) & (j == k)
    out_ref[...] = jnp.where(same & (late | alone), 1.0, 0.0).astype(BF)


def rms(values, gain):
    scale = lax.rsqrt(jnp.mean(values * values, axis=-1, keepdims=True) + eps)
    return (values * scale * gain).astype(BF)


def fill_tokens(tokens_ref, pieces):
    half = TOKENS // 2
    for side in range(2):
        mine = pieces[5 * side : 5 * side + 5]
        for place in range(3):
            tokens_ref[side * TS + place] = mine[place][...]
        tokens_ref[side * TS + 3, :half] = mine[3][...]
        tokens_ref[side * TS + 3, half:] = mine[4][...]


def product(tokens_ref, weight, start):
    depth = weight.shape[0]
    columns = pl.ds(pl.multiple_of(start, HEAD), depth)
    return dot(tokens_ref[:, :, columns].reshape(2 * TS * TOKENS, depth), weight[...])


def qkv_kernel(*refs):
    weights, (qkv_ref, tokens_ref) = refs[10:13], refs[13:]
    fill_tokens(tokens_ref, refs[:10])
    y = lax.axis_index("y")
    for place, weight in enumerate(weights):
        term = product(tokens_ref, weight, lax.rem(y + AWAY[place], NY) * WIDE)
        if place == 0:
            qkv_ref[...] = term
        else:
            qkv_ref[...] += term


def attend_kernel(*refs):
    weights = refs[10:12]
    partial_ref, qg_ref, kg_ref, att_ref, tokens_ref, qkv_ref = refs[12:]
    fill_tokens(tokens_ref, refs[:10])
    start = lax.rem(lax.axis_index("y") + 2, NY) * WIDE
    qkv_ref[...] = partial_ref[...] + product(tokens_ref, weights[0], start)
    qkv_ref[...] += product(tokens_ref, weights[1], start + WIDE // 2)

    def part(index, column):
        here = slice(column * HEAD, (column + 1) * HEAD)
        first, second = index * TOKENS, (TS + index) * TOKENS
        return jnp.concatenate(
            [qkv_ref[first : first + TOKENS, here], qkv_ref[second : second + TOKENS, here]], 0
        )

    for index in range(TS):
        for head in range(2):
            queries = rms(part(index, 3 * head), qg_ref[...])
            keys = rms(part(index, 3 * head + 1), kg_ref[...])
            values = part(index, 3 * head + 2).astype(BF)
            scores = dot_t(queries, keys) * (1.0 / math.sqrt(HEAD))
            scores = jnp.exp(scores - jnp.max(scores, axis=-1, keepdims=True))
            share = scores / jnp.sum(scores, axis=-1, keepdims=True)
            result = dot(share.astype(BF), values).astype(BF)
            at = head * HEAD
            att_ref[0, index, :, at : at + HEAD] = result[:TOKENS]
            att_ref[1, index, :, at : at + HEAD] = result[TOKENS:]


def project_kernel(steps_ref, offset_ref, mod_ref, *refs):
    att, sib, blocks = refs[0:5], refs[5:10], refs[10:15]
    state_ref, perm_ref, out_ref, weight_ref = refs[15:]
    y, x, h, z, core = (lax.axis_index(a) for a in AXES)
    plans = mod_ref.shape[1]

    for place, block in enumerate(blocks):
        source = lax.rem(y + AWAY[min(place, 3)], NY)
        into = lax.rem(source, 2)
        down = pl.multiple_of((source >> 1) * (COLS // 2), 16)
        zs = {3: (0, 1), 4: (2, 3)}.get(place, range(NZ))
        for at, zz in enumerate(zs):
            rows = COLS // 2
            weight_ref[into, zz, pl.ds(down, rows)] = block[at * rows : (at + 1) * rows]

    def piece(pieces, place, half):
        if place < 3:
            return pieces[place][half].reshape(TS * TOKENS, 2 * HEAD)
        return pieces[3 + half][...].reshape(TS * TOKENS, 2 * HEAD)

    column = pl.multiple_of((x * NC + core) * COLS, HEAD)
    for half in range(2):
        totals = [None] * TS
        for place, away in enumerate(AWAY):
            group = lax.rem(x + away, NX)
            term = dot_t(piece(att, place, half), weight_ref[core, group])
            term += dot_t(piece(sib, place, 1 - half), weight_ref[1 - core, group])
            for j in range(TS):
                at = AWAY.index((j - away) % NX) * TOKENS
                rows = term[at : at + TOKENS]
                totals[j] = rows if totals[j] is None else totals[j] + rows
        token_core = core if half == 0 else 1 - core
        values = []
        for j in range(TS):
            there = lax.rem(x + j, NX)
            k = step_index(y, there, h)
            now = steps_ref[k]
            size = (now - steps_ref[k + 1]).astype(F32) / plans
            first = jnp.where(k == offset_ref[z], 1.0, 0.0)
            gate = mod_ref[2, pl.ds(now, 1), pl.ds(column, COLS)]
            state = state_ref[there, :, token_core].reshape(TOKENS, COLS).astype(F32)
            increment = size * (state + gate * totals[j])
            values.append((increment + first * state).astype(BF).reshape(NZ, ROWS, COLS))
        for zz in range(NZ):
            stacked = jnp.concatenate([v[zz] for v in values], 0)
            moved = dot(perm_ref[...], stacked).astype(BF)
            out_ref[:, zz, token_core] = moved.reshape(NY * NH, TS * 4, COLS)


def prefix_kernel(lower_ref, terms_ref, out_ref):
    for c in range(NC):
        terms = terms_ref[:, c].reshape(NY * NH * SEQS * 16, COLS)
        total = dot(lower_ref[...], terms).astype(BF)
        out_ref[:, :, c * COLS : (c + 1) * COLS] = total.reshape(32, 16, COLS)


def leave_kernel(offset_ref, got_ref, cur_ref, perm_ref, out_ref):
    got = got_ref[:, 0].reshape(NY * NH * 16, 2 * COLS)
    total = dot(perm_ref[...], got).reshape(SEQS, ROWS, 2 * COLS)
    mine = my_step()
    for s in range(SEQS):
        out_ref[0, s] = total[s] + jnp.where(mine < offset_ref[s], cur_ref[0, s], 0.0)


def row_orders():
    out = np.zeros((128, 128), np.float32)
    for part in range(8):
        for a in range(4):
            for t in range(4):
                out[part * 16 + a * 4 + t, a * 32 + part * 4 + t] = 1
    return jnp.asarray(out, BF), jnp.asarray(out.T, BF)


def shape(*dims, kind=BF):
    return jax.ShapeDtypeStruct(dims, kind)


def body(trajectory, timesteps, offset, mod_table, w_qkv, w_out, query_gain, k_gain):
    planes = mod_table.transpose(1, 0, 2)
    wq = lax.ppermute(w_qkv, AXES, TO_HEADS)
    wo = lax.ppermute(w_out.T, AXES, TO_COLUMNS)
    hidden, state = call(
        enter_kernel,
        (shape(SEQS, ROWS, D), shape(NX, SEQS, NC, ROWS, COLS)),
        [SMEM, HBM, HBM],
        mib=58,
        out_specs=(VMEM, VMEM),
        scratch_shapes=[
            pltpu.VMEM((SEQS, ROWS, D), F32),
            pltpu.VMEM((2,) + planes.shape[1:], F32),
            pltpu.SemaphoreType.DMA((SEQS + 1,)),
        ],
    )(timesteps, trajectory, planes)
    lower = call(lower_kernel, shape(512, 512), [SMEM], out_specs=VMEM)(offset)

    tokens = lax.all_to_all(hidden, "z", 0, 0)
    wq = spread(after(wq, tokens), ("z", "h"), NZ * NH).reshape(WIDE, 6 * HEAD)
    weights = ring_rows(wq, "y", NY)
    tokens = ring_rows(tokens.reshape(TOKENS, D), "x", NX)
    others = tuple(other_core(v) for v in tokens)

    wo = spread(after(wo, wq), ("z", "h"), NZ * NH).reshape(NZ * NH * 96, 2 * HEAD)
    state = lax.all_to_all(
        after(state, (wo, tokens[3], tokens[4])).reshape(NX * SEQS * NC, ROWS, COLS), ("x", "z", "c"), 0, 0
    ).reshape(NX, NZ, NC, ROWS, COLS)
    columns = ring_rows(wo, "y", NY)

    scratch = [pltpu.VMEM((2 * TS, TOKENS, D), BF)]
    partial = call(
        qkv_kernel,
        shape(2 * TS * TOKENS, 6 * HEAD, kind=F32),
        [VMEM] * 13,
        out_specs=VMEM,
        scratch_shapes=scratch,
    )(*tokens, *others, *weights[:3])
    attended = call(
        attend_kernel,
        shape(2, TS, TOKENS, 2 * HEAD),
        [VMEM] * 15,
        out_specs=VMEM,
        scratch_shapes=scratch + [pltpu.VMEM((2 * TS * TOKENS, 6 * HEAD), F32)],
    )(*tokens, *others, *weights[3:], partial, query_gain[None], k_gain[None])

    attended = ring(after(attended, state), "x", NX, lambda b: b[0], lambda b: b[1])
    sibling = tuple(other_core(v) for v in attended)

    outward, back = row_orders()
    terms = call(
        project_kernel,
        shape(NY * NH, NZ, NC, TS * 4, COLS),
        [SMEM, SMEM] + [VMEM] * 18,
        out_specs=VMEM,
        scratch_shapes=[pltpu.VMEM((NC, NZ, COLS, 2 * HEAD), BF)],
    )(timesteps, offset, planes, *attended, *sibling, *columns, state, outward)
    terms = lax.all_to_all(terms.reshape(64, TS * 4, COLS), ("y", "h", "z", "c"), 0, 0)
    sums = call(prefix_kernel, shape(32, 16, 2 * COLS), [VMEM, VMEM], out_specs=VMEM)(
        lower, terms.reshape(32, NC, 16, COLS)
    )
    got = lax.all_to_all(sums, ("y", "x", "h"), 0, 0)
    return call(
        leave_kernel,
        shape(1, SEQS, ROWS, D, kind=F32),
        [
            SMEM,
            pl.BlockSpec((NY, 1, NH, 16, 2 * COLS), lambda i: (0, i, 0, 0, 0)),
            pl.BlockSpec((1, SEQS, ROWS, 2 * COLS), lambda i: (0, 0, 0, i)),
            pl.BlockSpec((128, 128), lambda i: (0, 0)),
        ],
        grid=(NX,),
        out_specs=pl.BlockSpec((1, SEQS, ROWS, 2 * COLS), lambda i: (0, 0, 0, i)),
    )(offset, got.reshape(NY, NX, NH, 16, 2 * COLS), trajectory, back)


def solution(mesh):
    fine = Mesh(mesh.devices.reshape(NY, NX, NH, NZ, NC), AXES)
    steps, places = ("y", "x", "h"), ("z", "c")
    return jax.shard_map(
        body,
        mesh=fine,
        in_specs=(
            P(steps, None, places, None),
            P(),
            P(),
            P(),
            P(steps, places),
            P(places, steps),
            P(),
            P(),
        ),
        out_specs=P(steps, None, places, None),
        check_vma=False,
    )
```

```python
import math

import jax
import jax.numpy as jnp
import numpy as np
from jax import lax
from jax.experimental import pallas as pl
from jax.experimental.pallas import tpu as pltpu
from jax.sharding import Mesh, PartitionSpec as P

eps = 1e-06
AXES = ("y", "x", "h", "z", "c")
NY, NX, NH, NZ, NC = 4, 4, 2, 4, 2
D = 3072
SEQS = 4
ROWS = 32
HEAD = 128
COLS = D // (NX * NC)
TS = 4
WIDE = D // NY
TOKENS = NZ * ROWS
AWAY = (0, 3, 1, 2)
BF = jnp.bfloat16
F32 = jnp.float32
SMEM = pl.BlockSpec(memory_space=pltpu.SMEM)
VMEM = pl.BlockSpec(memory_space=pltpu.VMEM)
HBM = pl.BlockSpec(memory_space=pltpu.HBM)


def flat(y, x, h, z, c):
    return (((y * NX + x) * NH + h) * NZ + z) * NC + c


def every():
    for y in range(NY):
        for x in range(NX):
            for h in range(NH):
                for z in range(NZ):
                    for c in range(NC):
                        yield y, x, h, z, c


TO_HEADS = [(flat(y, x, h, z, c), flat(y, z, h, x, c)) for y, x, h, z, c in every()]
TO_COLUMNS = [
    (flat(y, x, h, z, c), flat((x % 2) * 2 + c, y, h, z, x // 2)) for y, x, h, z, c in every()
]


def spread(v, axes, parts):
    copies = jnp.broadcast_to(v[None], (parts,) + v.shape)
    return lax.all_to_all(copies, axes, 0, 0)


def other_core(v):
    return lax.ppermute(v, "c", [(0, 1), (1, 0)])


def shift(v, axis, size, away):
    return lax.ppermute(v, axis, [(i, (i + away) % size) for i in range(size)])


def ring(v, axis, size, first, second):
    before = shift(v, axis, size, 1)
    after_ = shift(v, axis, size, -1)
    far = (shift(first(before), axis, size, 1), shift(second(after_), axis, size, -1))
    return (v, before, after_) + far


def ring_rows(v, axis, size):
    n = v.shape[0] // 2
    return ring(v, axis, size, lambda b: b[:n], lambda b: b[n:])


def after(v, other):
    return lax.optimization_barrier((v, other))[0]


def call(kernel, out_shape, specs, mib=48, **rest):
    return pl.pallas_call(
        kernel,
        out_shape=out_shape,
        in_specs=specs,
        compiler_params=pltpu.CompilerParams(vmem_limit_bytes=mib * 1024 * 1024),
        **rest,
    )


def dot(a, b):
    return lax.dot_general(a, b, (((1,), (0,)), ((), ())), preferred_element_type=F32)


def dot_t(a, b):
    return lax.dot_general(a, b, (((1,), (1,)), ((), ())), preferred_element_type=F32)


def step_index(y, x, h):
    return (y * NX + x) * NH + h


def my_step():
    return step_index(lax.axis_index("y"), lax.axis_index("x"), lax.axis_index("h"))


def enter_kernel(steps_ref, cur_hbm, mod_hbm, hidden_ref, state_ref, cur_ref, mod_ref, sems):
    plane = pltpu.make_async_copy(mod_hbm.at[0:2], mod_ref, sems.at[SEQS])
    loads = [
        pltpu.make_async_copy(cur_hbm.at[0, s], cur_ref.at[s], sems.at[s]) for s in range(SEQS)
    ]
    for copy in loads + [plane]:
        copy.start()
    now = steps_ref[my_step()]
    for s in range(SEQS):
        loads[s].wait()
        values = cur_ref[s]
        mean = jnp.mean(values, axis=-1, keepdims=True)
        centered = values - mean
        variance = jnp.mean(centered * centered, axis=-1, keepdims=True)
        cur_ref[s] = centered * lax.rsqrt(variance + eps)
        for x in range(NX):
            for c in range(NC):
                at = (x * NC + c) * COLS
                state_ref[x, s, c] = values[:, at : at + COLS].astype(BF)
    plane.wait()
    shift_row = mod_ref[0, pl.ds(now, 1), :]
    scale_row = 1.0 + mod_ref[1, pl.ds(now, 1), :]
    for s in range(SEQS):
        hidden_ref[s] = (cur_ref[s] * scale_row + shift_row).astype(BF)


def lower_kernel(offset_ref, out_ref):
    shape = (512, 512)
    row = lax.broadcasted_iota(jnp.int32, shape, 0)
    col = lax.broadcasted_iota(jnp.int32, shape, 1)
    bits = lambda v, at, n: (v >> at) & ((1 << n) - 1)
    k, s, t = row >> 4, bits(row, 2, 2), bits(row, 0, 2)
    y, h, s2 = col >> 7, bits(col, 6, 1), bits(col, 4, 2)
    x = (bits(col, 2, 2) + lax.axis_index("x")) & (NX - 1)
    j = step_index(y, x, h)
    start = jnp.full(shape, offset_ref[0], jnp.int32)
    for index in range(1, SEQS):
        start = jnp.where(s == index, offset_ref[index], start)
    same = (s == s2) & (t == bits(col, 0, 2))
    late = (k >= start) & (j >= start) & (j <= k)
    alone = (k < start) & (j == k)
    out_ref[...] = jnp.where(same & (late | alone), 1.0, 0.0).astype(BF)


def rms(values, gain):
    scale = lax.rsqrt(jnp.mean(values * values, axis=-1, keepdims=True) + eps)
    return (values * scale * gain).astype(BF)


def fill_tokens(tokens_ref, pieces):
    half = TOKENS // 2
    for side in range(2):
        mine = pieces[5 * side : 5 * side + 5]
        for place in range(3):
            tokens_ref[side * TS + place] = mine[place][...]
        tokens_ref[side * TS + 3, :half] = mine[3][...]
        tokens_ref[side * TS + 3, half:] = mine[4][...]


def product(tokens_ref, weight, start):
    depth = weight.shape[0]
    columns = pl.ds(pl.multiple_of(start, HEAD), depth)
    return dot(tokens_ref[:, :, columns].reshape(2 * TS * TOKENS, depth), weight[...])


def qkv_kernel(*refs):
    weights, (qkv_ref, tokens_ref) = refs[10:13], refs[13:]
    fill_tokens(tokens_ref, refs[:10])
    y = lax.axis_index("y")
    for place, weight in enumerate(weights):
        term = product(tokens_ref, weight, lax.rem(y + AWAY[place], NY) * WIDE)
        if place == 0:
            qkv_ref[...] = term
        else:
            qkv_ref[...] += term


def attend_kernel(*refs):
    mine, others, weights = refs[0:5], refs[5:10], refs[10:12]
    partial_ref, qg_ref, kg_ref, att_ref, tokens_ref, weight_ref, qkv_ref = refs[12:]
    half = TOKENS // 2
    start = lax.rem(lax.axis_index("y") + 2, NY) * WIDE
    columns = pl.ds(pl.multiple_of(start, HEAD), WIDE)
    for side, pieces in enumerate((mine, others)):
        for place in range(3):
            tokens_ref[side * TS + place] = pieces[place][:, columns]
        tokens_ref[side * TS + 3, :half] = pieces[3][:, columns]
        tokens_ref[side * TS + 3, half:] = pieces[4][:, columns]
    weight_ref[: WIDE // 2] = weights[0][...]
    weight_ref[WIDE // 2 :] = weights[1][...]
    tokens = tokens_ref[...].reshape(2 * TS * TOKENS, WIDE)
    qkv_ref[...] = partial_ref[...] + dot(tokens, weight_ref[...])

    def part(index, column):
        here = slice(column * HEAD, (column + 1) * HEAD)
        first, second = index * TOKENS, (TS + index) * TOKENS
        return jnp.concatenate(
            [qkv_ref[first : first + TOKENS, here], qkv_ref[second : second + TOKENS, here]], 0
        )

    for index in range(TS):
        for head in range(2):
            queries = rms(part(index, 3 * head), qg_ref[...])
            keys = rms(part(index, 3 * head + 1), kg_ref[...])
            values = part(index, 3 * head + 2).astype(BF)
            scores = dot_t(queries, keys)
            scores = scores - jnp.max(scores, axis=-1, keepdims=True)
            scores = jnp.exp2(scores * (math.log2(math.e) / math.sqrt(HEAD)))
            share = scores * (1.0 / jnp.sum(scores, axis=-1, keepdims=True))
            result = dot(share.astype(BF), values).astype(BF)
            at = head * HEAD
            att_ref[0, index, :, at : at + HEAD] = result[:TOKENS]
            att_ref[1, index, :, at : at + HEAD] = result[TOKENS:]


def project_kernel(steps_ref, offset_ref, mod_ref, *refs):
    att, sib, blocks = refs[0:5], refs[5:10], refs[10:15]
    state_ref, perm_ref, out_ref, weight_ref = refs[15:]
    y, x, h, z, core = (lax.axis_index(a) for a in AXES)
    plans = mod_ref.shape[1]

    for place, block in enumerate(blocks):
        source = lax.rem(y + AWAY[min(place, 3)], NY)
        into = lax.rem(source, 2)
        down = pl.multiple_of((source >> 1) * (COLS // 2), 16)
        zs = {3: (0, 1), 4: (2, 3)}.get(place, range(NZ))
        for at, zz in enumerate(zs):
            rows = COLS // 2
            weight_ref[into, zz, pl.ds(down, rows)] = block[at * rows : (at + 1) * rows]

    def piece(pieces, place, half):
        if place < 3:
            return pieces[place][half].reshape(TS * TOKENS, 2 * HEAD)
        return pieces[3 + half][...].reshape(TS * TOKENS, 2 * HEAD)

    column = pl.multiple_of((x * NC + core) * COLS, HEAD)
    for half in range(2):
        totals = [None] * TS
        for place, away in enumerate(AWAY):
            group = lax.rem(x + away, NX)
            term = dot_t(piece(att, place, half), weight_ref[core, group])
            term += dot_t(piece(sib, place, 1 - half), weight_ref[1 - core, group])
            for j in range(TS):
                at = AWAY.index((j - away) % NX) * TOKENS
                rows = term[at : at + TOKENS]
                totals[j] = rows if totals[j] is None else totals[j] + rows
        token_core = core if half == 0 else 1 - core
        values = []
        for j in range(TS):
            there = lax.rem(x + j, NX)
            k = step_index(y, there, h)
            now = steps_ref[k]
            size = (now - steps_ref[k + 1]).astype(F32) / plans
            first = jnp.where(k == offset_ref[z], 1.0, 0.0)
            gate = mod_ref[2, pl.ds(now, 1), pl.ds(column, COLS)]
            state = state_ref[there, :, token_core].reshape(TOKENS, COLS).astype(F32)
            increment = size * (state + gate * totals[j])
            values.append((increment + first * state).astype(BF).reshape(NZ, ROWS, COLS))
        for zz in range(NZ):
            stacked = jnp.concatenate([v[zz] for v in values], 0)
            moved = dot(perm_ref[...], stacked).astype(BF)
            out_ref[:, zz, token_core] = moved.reshape(NY * NH, TS * 4, COLS)


def prefix_kernel(lower_ref, terms_ref, out_ref):
    for c in range(NC):
        terms = terms_ref[:, c].reshape(NY * NH * SEQS * 16, COLS)
        total = dot(lower_ref[...], terms).astype(BF)
        out_ref[:, :, c * COLS : (c + 1) * COLS] = total.reshape(32, 16, COLS)


def leave_kernel(offset_ref, got_ref, cur_ref, perm_ref, out_ref):
    got = got_ref[:, 0].reshape(NY * NH * 16, 2 * COLS)
    total = dot(perm_ref[...], got).reshape(SEQS, ROWS, 2 * COLS)
    mine = my_step()
    for s in range(SEQS):
        out_ref[0, s] = total[s] + jnp.where(mine < offset_ref[s], cur_ref[0, s], 0.0)


def row_orders():
    out = np.zeros((128, 128), np.float32)
    for part in range(8):
        for a in range(4):
            for t in range(4):
                out[part * 16 + a * 4 + t, a * 32 + part * 4 + t] = 1
    return jnp.asarray(out, BF), jnp.asarray(out.T, BF)


def shape(*dims, kind=BF):
    return jax.ShapeDtypeStruct(dims, kind)


def body(trajectory, timesteps, offset, mod_table, w_qkv, w_out, query_gain, k_gain):
    planes = mod_table.transpose(1, 0, 2)
    wq = lax.ppermute(w_qkv, AXES, TO_HEADS)
    wo = lax.ppermute(w_out.T, AXES, TO_COLUMNS)
    hidden, state = call(
        enter_kernel,
        (shape(SEQS, ROWS, D), shape(NX, SEQS, NC, ROWS, COLS)),
        [SMEM, HBM, HBM],
        mib=58,
        out_specs=(VMEM, VMEM),
        scratch_shapes=[
            pltpu.VMEM((SEQS, ROWS, D), F32),
            pltpu.VMEM((2,) + planes.shape[1:], F32),
            pltpu.SemaphoreType.DMA((SEQS + 1,)),
        ],
    )(timesteps, trajectory, planes)
    lower = call(lower_kernel, shape(512, 512), [SMEM], out_specs=VMEM)(offset)

    tokens = lax.all_to_all(hidden, "z", 0, 0)
    wq = spread(after(wq, tokens), ("z", "h"), NZ * NH).reshape(WIDE, 6 * HEAD)
    weights = ring_rows(wq, "y", NY)
    tokens = ring_rows(tokens.reshape(TOKENS, D), "x", NX)
    others = tuple(other_core(v) for v in tokens)

    wo = spread(after(wo, wq), ("z", "h"), NZ * NH).reshape(NZ * NH * 96, 2 * HEAD)
    state = lax.all_to_all(
        after(state, (wo, tokens[3], tokens[4])).reshape(NX * SEQS * NC, ROWS, COLS), ("x", "z", "c"), 0, 0
    ).reshape(NX, NZ, NC, ROWS, COLS)
    columns = ring_rows(wo, "y", NY)

    scratch = [pltpu.VMEM((2 * TS, TOKENS, D), BF)]
    partial = call(
        qkv_kernel,
        shape(2 * TS * TOKENS, 6 * HEAD, kind=F32),
        [VMEM] * 13,
        out_specs=VMEM,
        scratch_shapes=scratch,
    )(*tokens, *others, *weights[:3])
    attended = call(
        attend_kernel,
        shape(2, TS, TOKENS, 2 * HEAD),
        [VMEM] * 15,
        out_specs=VMEM,
        scratch_shapes=[
            pltpu.VMEM((2 * TS, TOKENS, WIDE), BF),
            pltpu.VMEM((WIDE, 6 * HEAD), BF),
            pltpu.VMEM((2 * TS * TOKENS, 6 * HEAD), F32),
        ],
    )(*tokens, *others, *weights[3:], partial, query_gain[None], k_gain[None])

    attended = ring(after(attended, state), "x", NX, lambda b: b[0], lambda b: b[1])
    sibling = tuple(other_core(v) for v in attended)

    outward, back = row_orders()
    terms = call(
        project_kernel,
        shape(NY * NH, NZ, NC, TS * 4, COLS),
        [SMEM, SMEM] + [VMEM] * 18,
        out_specs=VMEM,
        scratch_shapes=[pltpu.VMEM((NC, NZ, COLS, 2 * HEAD), BF)],
    )(timesteps, offset, planes, *attended, *sibling, *columns, state, outward)
    terms = lax.all_to_all(terms.reshape(64, TS * 4, COLS), ("y", "h", "z", "c"), 0, 0)
    sums = call(prefix_kernel, shape(32, 16, 2 * COLS), [VMEM, VMEM], out_specs=VMEM)(
        lower, terms.reshape(32, NC, 16, COLS)
    )
    got = lax.all_to_all(sums, ("y", "x", "h"), 0, 0)
    return call(
        leave_kernel,
        shape(1, SEQS, ROWS, D, kind=F32),
        [
            SMEM,
            pl.BlockSpec((NY, 1, NH, 16, 2 * COLS), lambda i: (0, i, 0, 0, 0)),
            pl.BlockSpec((1, SEQS, ROWS, 2 * COLS), lambda i: (0, 0, 0, i)),
            pl.BlockSpec((128, 128), lambda i: (0, 0)),
        ],
        grid=(NX,),
        out_specs=pl.BlockSpec((1, SEQS, ROWS, 2 * COLS), lambda i: (0, 0, 0, i)),
    )(offset, got.reshape(NY, NX, NH, 16, 2 * COLS), trajectory, back)


def solution(mesh):
    fine = Mesh(mesh.devices.reshape(NY, NX, NH, NZ, NC), AXES)
    steps, places = ("y", "x", "h"), ("z", "c")
    return jax.shard_map(
        body,
        mesh=fine,
        in_specs=(
            P(steps, None, places, None),
            P(),
            P(),
            P(),
            P(steps, places),
            P(places, steps),
            P(),
            P(),
        ),
        out_specs=P(steps, None, places, None),
        check_vma=False,
    )
```
